32 devices in a mesh: ctx: 8 (over z, x), tp: 4 (over y, core).
Axes of the slice: x: 2, y: 2, z: 4, core: 2. Of those that a mesh axis runs over, the one named last changes fastest.
Arguments:
- queries: bfloat16 [4096, 8192], P('ctx', 'tp'), may hold values from -23 to 23
- keys: bfloat16 [4096, 1024], P('ctx', 'tp'), may hold values from -23 to 23
- values: bfloat16 [4096, 1024], P('ctx', 'tp'), may hold values from -6 to 6
- grad_out: bfloat16 [4096, 8192], P('ctx', 'tp'), may hold values from -6 to 6
- doc_ids: int32 [4096], P(('ctx', 'tp')), may hold values from 0 to 7, never falling along the last dimension, each value on 1 to 2048 neighbouring positions
Outputs:
- attended: bfloat16 [4096, 8192], P('ctx', 'tp')
- grad_queries: bfloat16 [4096, 8192], P('ctx', 'tp')
- grad_keys: bfloat16 [4096, 1024], P('ctx', 'tp')
- grad_values: bfloat16 [4096, 1024], P('ctx', 'tp')
The draws below stay inside these ranges and needn't reach their ends.
Inputs may be any that keep to these rules, and one draw needn't show every extreme that they name: `doc_ids`: ids never fall along the pack; each document holds 1 to 2048 tokens, one exactly 2048.
All inputs are finite; a program needn't handle non-finite values.
Results may differ from the reference program's by a relative error of at most 0.035.
Values may be sent and summed in bfloat16 or wider, within the bound.
No kernel may reach another device: no remote copies, remote signals or barrier semaphores. Data moves between devices by JAX's collectives and lax.ppermute only.
A program may use at most 128 MiB of HBM per device.

```python
import math
import jax
import jax.numpy as jnp
import numpy as np
from jax import lax

HD = 128
QH = 64
KVH = 8
TOK_DEV = 512
TOKENS = 4096
MOST = 2048
DOCS = 8


def shared_keys(key):
    base = jnp.clip(jax.random.normal(key, (TOKENS, KVH * HD), jnp.float32), -5.0, 5.0)
    return base


def draw_keys(key, part):
    base = shared_keys(key)
    result = base
    return result.astype(jnp.bfloat16)


def draw_queries(key, part):
    key = jax.random.fold_in(key, 12)
    result = jnp.clip(jax.random.normal(key, (TOKENS, QH * HD), jnp.float32), -5.0, 5.0)
    return result.astype(jnp.bfloat16)


def block_scale(stream_key, dims, split, least, largest):
    gain, own = 1.0, jax.random.fold_in(stream_key, 6)
    for dim, shards_of in split:
        draws = jnp.exp(jax.random.uniform(jax.random.fold_in(own, dim), (shards_of,), jnp.float32, least / len(split), largest / len(split)))
        gain = gain * jnp.repeat(draws, dims[dim] // shards_of).reshape([-1 if axis == dim else 1 for axis in range(len(dims))])
    return gain


def split_up(count, total, bound, slope):
    portions = [(1 << 20) // math.isqrt(grade ** slope) + 1 for grade in range(2, count + 1)]
    spare, holding = total - bound - (count - 1), [1] * (count - 1)
    while spare > 0:
        candidates = [i for i in range(count - 1) if holding[i] < bound]
        whole, remaining = sum([portions[i] for i in candidates]), spare
        for i in candidates:
            addition = min(bound - holding[i], max(1, remaining * portions[i] // whole), spare)
            holding[i] = holding[i] + addition
            spare = spare - addition
    return np.array([bound] + holding)


def uneven_parts(stream_key, number_of, total, most, slope):
    if number_of == 2:
        one = jax.random.randint(stream_key, (), max(1, total - most), min(most, total - 1) + 1)
        return jnp.stack([one, total - one])
    tallies = jnp.asarray(split_up(number_of, total, most, slope), jnp.int32)
    pairs = (number_of - 1) // 2
    donor, sink = tallies[1:1 + 2 * pairs:2], tallies[2:2 + 2 * pairs:2]
    slack = jnp.minimum(donor - 1, most - sink)
    moved = jax.random.randint(jax.random.fold_in(stream_key, 1), (pairs,), 0, 1 << 20) % (slack + 1)
    tallies = tallies.at[1:1 + 2 * pairs:2].set(donor - moved).at[2:2 + 2 * pairs:2].set(sink + moved)
    return tallies[jax.random.permutation(jax.random.fold_in(stream_key, 2), number_of)]


def scatter_about(stream_key, extent, scale, most, split=(), held_as=jnp.bfloat16):
    array = scale * jax.random.normal(stream_key, extent, jnp.float32)
    if split:
        array = array * block_scale(stream_key, extent, split, -0.22, 0.18)
    return jnp.clip(array, -most, most).astype(held_as)


def setup_inputs(seed: int = 0) -> dict:
    seeds = jax.random.split(jax.random.key(seed), 6)
    queries = draw_queries(jax.random.fold_in(seeds[5], 71), 0)
    keys = draw_keys(jax.random.fold_in(seeds[5], 71), 0)
    values = scatter_about(seeds[2], (TOKENS, KVH * HD), 1.0, 6.0, ((0, 8), (1, 4)))
    grad_out = scatter_about(seeds[3], (TOKENS, QH * HD), 1.0, 6.0, ((0, 8), (1, 4)))
    doc_ids = jnp.searchsorted(jnp.cumsum(uneven_parts(seeds[4], DOCS, TOKENS, MOST, 2)), jnp.arange(TOKENS), side="right").astype(jnp.int32)
    return {"queries": queries, "keys": keys, "values": values, "grad_out": grad_out, "doc_ids": doc_ids}


NEG = -1e+30

def tile_mask(query_docs, key_docs, query_pos, key_pos):
    same = query_docs[:, None] == key_docs[None, :]
    before = key_pos[None, :] <= query_pos[:, None]
    return (same & before)[None, None]

def tile_scores(q_tile, k_tile):
    return jnp.einsum('qkgd,jkd->kgqj', q_tile.astype(jnp.float32), k_tile.astype(jnp.float32)) * (1.0 / math.sqrt(HD))

def rounded(x):
    return lax.optimization_barrier(x.astype(jnp.bfloat16)).astype(jnp.float32)

def reference(queries, keys, values, grad_out, doc_ids):
    blk = TOK_DEV
    blocks = TOKENS // TOK_DEV
    group = QH // KVH
    reach = MOST // TOK_DEV
    scale = 1.0 / math.sqrt(HD)
    q_all = queries.reshape(blocks, blk, KVH, group, HD)
    g_all = grad_out.reshape(blocks, blk, KVH, group, HD)
    k_all = keys.reshape(blocks, blk, KVH, HD)
    v_all = values.reshape(blocks, blk, KVH, HD)
    ids_all = doc_ids.reshape(blocks, blk)
    offsets = jnp.arange(blk, dtype=jnp.int32)

    def locate(index, back):
        source = jnp.maximum(index - back, 0).astype(jnp.int32)
        live = (index - back >= 0) & (ids_all[index][0] <= ids_all[source][blk - 1])
        allowed = tile_mask(ids_all[index], ids_all[source], index * blk + offsets, source * blk + offsets)
        return (source, live, allowed)

    def per_block(carry, index):
        key_acc, value_acc = carry
        q_tile = q_all[index]
        g_tile = g_all[index]
        run_max = jnp.full((KVH, group, blk), NEG, jnp.float32)
        run_sum = jnp.zeros((KVH, group, blk), jnp.float32)
        for back in range(reach + 1):
            source, live, allowed = locate(index, back)

            def stats(unused):
                scores = tile_scores(q_tile, k_all[source])
                tile_max = lax.optimization_barrier(jnp.max(jnp.where(allowed, scores, NEG), axis=-1))
                tile_sum = lax.optimization_barrier(jnp.sum(jnp.where(allowed, jnp.exp(scores - tile_max[..., None]), 0.0), axis=-1))
                return (tile_max, tile_sum)

            def empty(unused):
                return (jnp.full((KVH, group, blk), NEG, jnp.float32), jnp.zeros((KVH, group, blk), jnp.float32))
            tile_max, tile_sum = lax.cond(live, stats, empty, 0)
            new_max = jnp.maximum(run_max, tile_max)
            run_sum = run_sum * jnp.exp(run_max - new_max) + tile_sum * jnp.exp(tile_max - new_max)
            run_max = new_max
        lse = run_max + jnp.log(run_sum)
        heads_out = jnp.zeros((KVH, group, blk, HD), jnp.float32)
        for back in range(reach + 1):
            source, live, allowed = locate(index, back)

            def forward(unused):
                scores = tile_scores(q_tile, k_all[source])
                probs = jnp.where(allowed, jnp.exp(scores - lse[..., None]), 0.0)
                return jnp.einsum('kgqj,jkd->kgqd', rounded(probs), v_all[source].astype(jnp.float32))

            def nothing(unused):
                return jnp.zeros((KVH, group, blk, HD), jnp.float32)
            heads_out = heads_out + lax.cond(live, forward, nothing, 0)
        attended = jnp.transpose(heads_out, (2, 0, 1, 3)).astype(jnp.bfloat16)
        delta = jnp.transpose(lax.optimization_barrier(jnp.sum(g_tile.astype(jnp.float32) * attended.astype(jnp.float32), axis=-1)), (1, 2, 0))
        grad_q = jnp.zeros((KVH, group, blk, HD), jnp.float32)
        for back in range(reach + 1):
            source, live, allowed = locate(index, back)

            def backward(unused):
                k_tile = k_all[source].astype(jnp.float32)
                v_tile = v_all[source].astype(jnp.float32)
                scores = tile_scores(q_tile, k_all[source])
                probs = jnp.where(allowed, jnp.exp(scores - lse[..., None]), 0.0)
                dprobs = jnp.einsum('qkgd,jkd->kgqj', g_tile.astype(jnp.float32), v_tile)
                dscores = rounded(probs * (dprobs - delta[..., None]) * scale)
                part_q = jnp.einsum('kgqj,jkd->kgqd', dscores, k_tile)
                part_k = jnp.einsum('kgqj,qkgd->jkd', dscores, q_tile.astype(jnp.float32))
                part_v = jnp.einsum('kgqj,qkgd->jkd', rounded(probs), g_tile.astype(jnp.float32))
                return (part_q, part_k, part_v)

            def skipped(unused):
                return (jnp.zeros((KVH, group, blk, HD), jnp.float32), jnp.zeros((blk, KVH, HD), jnp.float32), jnp.zeros((blk, KVH, HD), jnp.float32))
            part_q, part_k, part_v = lax.cond(live, backward, skipped, 0)
            grad_q = grad_q + part_q
            key_acc = key_acc.at[source].add(part_k)
            value_acc = value_acc.at[source].add(part_v)
        grad_tile = jnp.transpose(grad_q, (2, 0, 1, 3)).astype(jnp.bfloat16)
        return ((key_acc, value_acc), (attended, grad_tile))
    start = (jnp.zeros((blocks, blk, KVH, HD), jnp.float32), jnp.zeros((blocks, blk, KVH, HD), jnp.float32))
    carry, outs = lax.scan(per_block, start, jnp.arange(blocks, dtype=jnp.int32))
    key_acc, value_acc = carry
    attended, grad_tiles = outs
    return (attended.reshape(TOKENS, QH * HD), grad_tiles.reshape(TOKENS, QH * HD), key_acc.reshape(TOKENS, KVH * HD).astype(jnp.bfloat16), value_acc.reshape(TOKENS, KVH * HD).astype(jnp.bfloat16))
```

```python
import functools, math
import jax, jax.numpy as jnp
from jax import lax
from jax.sharding import PartitionSpec as P
from jax.experimental import pallas as pl
from jax.experimental.pallas import tpu as pltpu

HD = 128
KB = 256
NEG = -1e30
BIG = 1e30
F32, BF16 = jnp.float32, jnp.bfloat16


def dot(a, b):
    return lax.dot_general(a, b, (((1,), (0,)), ((), ())), preferred_element_type=F32)


def body(group, nkeys, first, lo_ref, q_ref, g_ref, kv_refs, start_ref, o_ref, dq_ref, dkv_ref,
         k_s, v_s, kt_s, vt_s, qt_s, gt_s, qs_s, gs_s, s_s, u_s, bias_s, db_s, ot_s, dqt_s, m_s, dk_s, dv_s):
    r = pl.program_id(0)
    rb = q_ref.shape[0]
    nb = nkeys // KB
    slab = kv_refs[0].shape[0]
    per = slab // KB
    c2 = math.log2(math.e) / math.sqrt(HD)

    @pl.when(r == 0)
    def _():
        for n, ref in enumerate(kv_refs):
            for t in range(per):
                j = n * per + t

                @pl.when(j >= lo_ref[0])
                def _():
                    k = ref[t * KB:(t + 1) * KB, :HD]
                    v = ref[t * KB:(t + 1) * KB, HD:]
                    k_s[j] = k
                    v_s[j] = v
                    kt_s[j] = k.T
                    vt_s[j, :HD] = v.T
                    vt_s[j, HD:] = jnp.ones((16, KB), BF16)
        dk_s[...] = jnp.zeros_like(dk_s)
        dv_s[...] = jnp.zeros_like(dv_s)

    for h in range(group):
        q = q_ref[:, h * HD:(h + 1) * HD]
        g = g_ref[:, h * HD:(h + 1) * HD]
        qs_s[h * rb:(h + 1) * rb, :] = q
        qt_s[:, h * rb:(h + 1) * rb] = q.T
        gt_s[:, h * rb:(h + 1) * rb] = g.T

    lo = lo_ref[r]
    hi = nb - pl.num_programs(0) * rb // KB + (r + 1) * rb // KB
    start = start_ref[0:1, :]
    qpos = (nkeys - pl.num_programs(0) * rb) + r * rb + lax.broadcasted_iota(jnp.int32, (1, rb), 1)
    dqt_s[...] = jnp.zeros_like(dqt_s)

    def set_bias(j):
        kpos = j * KB + lax.broadcasted_iota(jnp.int32, (KB, rb), 0)
        bias_s[...] = jnp.where((kpos >= start) & (kpos <= qpos), BIG, NEG)

    def scores(j, cols):
        return jnp.minimum(dot(k_s[j], qt_s[:, cols]), bias_s[...])

    def fold_max(s):
        return jnp.max(s.reshape(KB // 8, 8, rb), axis=0)

    def weigh(j, s, cols):
        u_s[j, :, cols] = jnp.exp2(s * c2 - m_s[0:1, cols]).astype(BF16)

    heads = [slice(h * rb, (h + 1) * rb) for h in range(group)]

    last = hi - 1
    set_bias(last)
    for cols in heads:
        s = scores(last, cols)
        s_s[:, cols] = s
        m_s[0:1, cols] = jnp.max(fold_max(s), axis=0, keepdims=True) * c2
    for cols in heads:
        weigh(last, s_s[:, cols], cols)
    ot_s[...] = dot(vt_s[last], u_s[last])

    @pl.loop(lo, last)
    def _(j):
        set_bias(j)
        for cols in heads:
            weigh(j, scores(j, cols), cols)
        ot_s[...] += dot(vt_s[j], u_s[j])

    @pl.when(jnp.logical_not(jnp.max(ot_s[HD:HD + 1, :]) < 2.0 ** 60))
    def _():
        m_s[...] = jnp.full_like(m_s, NEG)

        @pl.loop(lo, hi)
        def _(j):
            set_bias(j)
            for cols in heads:
                m_s[:, cols] = jnp.maximum(m_s[:, cols], fold_max(scores(j, cols)))

        m_s[0:1, :] = jnp.max(m_s[...], axis=0, keepdims=True) * c2
        ot_s[...] = jnp.zeros_like(ot_s)

        @pl.loop(lo, hi)
        def _(j):
            set_bias(j)
            for cols in heads:
                weigh(j, scores(j, cols), cols)
            ot_s[...] += dot(vt_s[j], u_s[j])

    rl = 1.0 / ot_s[HD:HD + 1, :]
    deltas = []
    for h in range(group):
        cols = slice(h * rb, (h + 1) * rb)
        ob = (ot_s[:HD, cols] * rl[:, cols]).astype(BF16)
        o_ref[:, h * HD:(h + 1) * HD] = ob.T
        gt = gt_s[:, cols].astype(F32) * rl[:, cols]
        deltas.append(jnp.sum(ob.astype(F32) * gt, axis=0, keepdims=True))
        gt = gt.astype(BF16)
        gt_s[:, cols] = gt
        gs_s[h * rb:(h + 1) * rb, :] = gt.T

    @pl.loop(lo, hi)
    def _(j):
        vj = v_s[j]
        for h in range(group):
            cols = slice(h * rb, (h + 1) * rb)
            dp = dot(vj, gt_s[:, cols])
            db_s[:, cols] = (u_s[j, :, cols].astype(F32) * (dp - deltas[h])).astype(BF16)
        dqt_s[...] += dot(kt_s[j], db_s[...])
        dk_s[j] += dot(db_s[...], qs_s[...])
        dv_s[j] += dot(u_s[j], gs_s[...])

    scale = 1.0 / math.sqrt(HD)
    for h in range(group):
        cols = slice(h * rb, (h + 1) * rb)
        dq_ref[:, h * HD:(h + 1) * HD] = (dqt_s[:, cols] * scale).astype(BF16).T

    @pl.when(r == pl.num_programs(0) - 1)
    def _():
        for j in range(nb):
            dkv_ref[j * KB:(j + 1) * KB, :HD] = (dk_s[j] * scale).astype(BF16)
            dkv_ref[j * KB:(j + 1) * KB, HD:] = dv_s[j].astype(BF16)


def attend(q, g, kvs, start, lo, chunk, group, prev=None, rb=256):
    rows, width = q.shape
    gw = group * HD
    slab = kvs[0].shape[0]
    nkeys = slab * len(kvs)
    nb = nkeys // KB
    R = group * rb
    n = len(kvs)

    def kernel(*refs):
        if prev is None:
            lo_ref, q_ref, g_ref, *rest = refs
        else:
            lo_ref, q_ref, g_ref, _, _, *rest = refs
        kv_refs, rest = rest[:n], rest[n:]
        body(group, nkeys, 0, lo_ref, q_ref, g_ref, kv_refs, *rest)

    blk = pl.BlockSpec((rb, gw), lambda r, lo: (r, chunk))
    extra = [] if prev is None else list(prev)
    return pl.pallas_call(
        kernel,
        grid_spec=pltpu.PrefetchScalarGridSpec(
            num_scalar_prefetch=1,
            grid=(rows // rb,),
            in_specs=[blk, blk] + [pl.BlockSpec(memory_space=pl.ANY)] * len(extra)
            + [pl.BlockSpec((slab, 2 * HD), lambda r, lo: (0, 0))] * n
            + [pl.BlockSpec((1, rb), lambda r, lo: (0, r))],
            out_specs=[blk, blk, pl.BlockSpec((nkeys, 2 * HD), lambda r, lo: (0, 0))],
            scratch_shapes=[
                pltpu.VMEM((nb, KB, HD), BF16), pltpu.VMEM((nb, KB, HD), BF16),
                pltpu.VMEM((nb, HD, KB), BF16), pltpu.VMEM((nb, HD + 16, KB), BF16),
                pltpu.VMEM((HD, R), BF16), pltpu.VMEM((HD, R), BF16),
                pltpu.VMEM((R, HD), BF16), pltpu.VMEM((R, HD), BF16),
                pltpu.VMEM((KB, R), F32), pltpu.VMEM((nb, KB, R), BF16),
                pltpu.VMEM((KB, rb), F32), pltpu.VMEM((KB, R), BF16),
                pltpu.VMEM((HD + 16, R), F32), pltpu.VMEM((HD, R), F32),
                pltpu.VMEM((8, R), F32),
                pltpu.VMEM((nb, KB, HD), F32), pltpu.VMEM((nb, KB, HD), F32),
            ],
        ),
        out_shape=[jax.ShapeDtypeStruct((rows, width), BF16), jax.ShapeDtypeStruct((rows, width), BF16),
                   jax.ShapeDtypeStruct((nkeys, 2 * HD), BF16)],
        input_output_aliases={} if prev is None else {3: 0, 4: 1},
        compiler_params=pltpu.CompilerParams(vmem_limit_bytes=56 * 1024 * 1024),
        name=f"attend{chunk}",
        cost_estimate=pl.CostEstimate(flops=40_000_000_000, bytes_accessed=10_000_000, transcendentals=0),
    )(lo, q, g, *extra, *kvs, start)
def hop(x, shift):
    count = lax.axis_size("ctx")
    return lax.ppermute(x, "ctx", [(s, s + shift) for s in range(count) if 0 <= s + shift < count])


def swap(x):
    return lax.ppermute(x, "ctx", [(s, s ^ 1) for s in range(lax.axis_size("ctx"))])


def after(x, *others):
    return lax.optimization_barrier((x,) + others)[0]


def gather_ids(doc_ids):
    tps = lax.axis_size("tp")
    ids = doc_ids[None]
    step = 1
    while step < tps:
        other = lax.ppermute(ids, "tp", [(t, t ^ step) for t in range(tps)])
        low = (lax.axis_index("tp") // step) % 2 == 0
        ids = jnp.where(low, jnp.concatenate([ids, other]), jnp.concatenate([other, ids]))
        step *= 2
    return ids.reshape(-1)


def on_device(queries, keys, values, grad_out, doc_ids):
    slab, width = keys.shape
    chunks = width // HD
    group = queries.shape[1] // width
    me = lax.axis_index("ctx")
    odd = lax.rem(me, 2) == 1
    rb = 256

    def own_part(c):
        return jnp.concatenate([keys[:, c * HD:(c + 1) * HD], values[:, c * HD:(c + 1) * HD]], axis=1)

    own = own_part(0)
    two = hop(own, 2)
    ids = gather_ids(doc_ids)
    two, ids_late = lax.optimization_barrier((two, ids))
    four = hop(two, 2)
    one = swap(jnp.where(odd, two, own))
    earlier = [jnp.where(me >= back, hop(ids, back), -1) for back in (4, 3, 2, 1)]
    four, earlier = lax.optimization_barrier((four, earlier))
    three = swap(jnp.where(odd, four, two))
    ready = (four, three)
    context = jnp.concatenate(earlier + [ids])
    start = jnp.sum((context[:, None] < ids[None, :]).astype(jnp.int32), axis=0)
    lo = start.reshape(slab // rb, rb)[:, 0] // KB
    start = start[None]
    blocks = [four, three, two, one, own]

    outs = None
    grads = []
    for c in range(chunks):
        following = None
        if c + 1 < chunks:
            own = after(own_part(c + 1), ready[0])
            two, own, _ = lax.optimization_barrier((hop(own, 2), own, ready[1]))
            following = [hop(two, 2), hop(two, 1), two, hop(own, 1), own]
        att, gq, parts = attend(queries, grad_out, blocks, start, lo, c, group, outs, rb)
        outs = (att, gq)
        four, three, two, one, own_grad = parts.reshape(5, slab, 2 * HD)
        if following is not None:
            back = [hop(four, -4), hop(three, -3), hop(two, -2), hop(one, -1)]
            grads.append([own_grad] + back)
        else:
            f32 = lambda x: x.astype(F32)
            three = after(three, *(x for part in grads for x in part))
            swap3 = f32(swap(three))
            swap1 = f32(swap(one))
            zero = jnp.zeros_like(swap3)
            four = (f32(four) + jnp.where(odd, swap3, zero)).astype(BF16)
            two = f32(two) + jnp.where(odd, swap1, swap3)
            two = (two + f32(hop(four, -2))).astype(BF16)
            grads.append([f32(own_grad) + jnp.where(odd, zero, swap1), hop(two, -2)])
        blocks = following
    sums = [sum(x.astype(F32) for x in parts) for parts in grads]
    grad_k = jnp.concatenate([x[:, :HD] for x in sums], axis=1).astype(BF16)
    grad_v = jnp.concatenate([x[:, HD:] for x in sums], axis=1).astype(BF16)
    return outs[0], outs[1], grad_k, grad_v


def solution(mesh):
    return jax.shard_map(
        on_device,
        mesh=mesh,
        in_specs=(P("ctx", "tp"), P("ctx", "tp"), P("ctx", "tp"), P("ctx", "tp"), P(("ctx", "tp"))),
        out_specs=(P("ctx", "tp"), P("ctx", "tp"), P("ctx", "tp"), P("ctx", "tp")),
        check_vma=False,
    )
```

```python
import functools, math
import jax, jax.numpy as jnp
from jax import lax
from jax.sharding import PartitionSpec as P
from jax.experimental import pallas as pl
from jax.experimental.pallas import tpu as pltpu

HD = 128
KB = 256
WIDTHS = (4, 2, 1)
NEG = -1e30
BIG = 1e30
F32, BF16 = jnp.float32, jnp.bfloat16


def dot(a, b):
    return lax.dot_general(a, b, (((1,), (0,)), ((), ())), preferred_element_type=F32)


def body(group, nkeys, lo_ref, q_ref, g_ref, kv_refs, start_ref, o_ref, dq_ref, dkv_refs,
         k_s, v_s, kt_s, vt_s, qt_s, gt_s, qs_s, gs_s, s_s, u_s, bias_s, db_s, ot_s, dqt_s, m_s, dk_s, dv_s):
    r = pl.program_id(0)
    rb = q_ref.shape[0]
    nb = nkeys // KB
    slab = kv_refs[0].shape[0]
    per = slab // KB
    c2 = math.log2(math.e) / math.sqrt(HD)

    @pl.when(r == 0)
    def _():
        for n, ref in enumerate(kv_refs):
            for t in range(per):
                at = slice((n * per + t) * KB, (n * per + t + 1) * KB)

                @pl.when(n * per + t >= lo_ref[0])
                def _():
                    k = ref[t * KB:(t + 1) * KB, :HD]
                    v = ref[t * KB:(t + 1) * KB, HD:]
                    k_s[at, :] = k
                    v_s[at, :] = v
                    kt_s[:, at] = k.T
                    vt_s[:HD, at] = v.T
        vt_s[HD:, :] = jnp.ones((vt_s.shape[0] - HD, nkeys), BF16)
        dk_s[...] = jnp.zeros_like(dk_s)
        dv_s[...] = jnp.zeros_like(dv_s)

    for h in range(group):
        q = q_ref[:, h * HD:(h + 1) * HD]
        g = g_ref[:, h * HD:(h + 1) * HD]
        qs_s[h * rb:(h + 1) * rb, :] = q
        qt_s[:, h * rb:(h + 1) * rb] = q.T
        gt_s[:, h * rb:(h + 1) * rb] = g.T

    lo = lo_ref[r]
    hi = nb - pl.num_programs(0) * rb // KB + (r + 1) * rb // KB
    start = start_ref[0:1, :]
    qpos = (nkeys - pl.num_programs(0) * rb) + r * rb + lax.broadcasted_iota(jnp.int32, (1, rb), 1)
    dqt_s[...] = jnp.zeros_like(dqt_s)

    def span(j, wide):
        return pl.ds(pl.multiple_of(j * KB, KB), wide * KB)

    def set_bias(j, wide):
        kpos = j * KB + lax.broadcasted_iota(jnp.int32, (wide * KB, rb), 0)
        bias_s[:wide * KB, :] = jnp.where((kpos >= start) & (kpos <= qpos), BIG, NEG)

    def scores(j, wide, cols):
        return jnp.minimum(dot(k_s[span(j, wide), :], qt_s[:, cols]), bias_s[:wide * KB, :])

    def fold_max(s):
        return jnp.max(s.reshape(KB // 8, 8, rb), axis=0)

    def weigh(j, wide, s, cols):
        u_s[span(j, wide), cols] = jnp.exp2(s * c2 - m_s[0:1, cols]).astype(BF16)

    def attend_step(j, wide):
        set_bias(j, wide)
        for cols in heads:
            weigh(j, wide, scores(j, wide, cols), cols)
        ot_s[...] += dot(vt_s[:, span(j, wide)], u_s[span(j, wide), :])

    def grad_step(j, wide):
        at = span(j, wide)
        for h, cols in enumerate(heads):
            dp = dot(v_s[at, :], gt_s[:, cols])
            db_s[:wide * KB, cols] = (u_s[at, cols].astype(F32) * (dp - deltas[h])).astype(BF16)
        db = db_s[:wide * KB, :]
        dqt_s[...] += dot(kt_s[:, at], db)
        dk_s[at, :] += dot(db, qs_s[...])
        dv_s[at, :] += dot(u_s[at, :], gs_s[...])

    def blocks(first, end, step):
        left = end - first
        for n, wide in enumerate(WIDTHS):
            if n == 0:
                count = left // wide

                @pl.loop(0, count)
                def _(i):
                    step(first + i * wide, wide)

                first, left = first + count * wide, left - count * wide
            else:
                take = left >= wide

                @pl.when(take)
                def _(first=first):
                    step(first, wide)

                first, left = first + jnp.where(take, wide, 0), left - jnp.where(take, wide, 0)

    heads = [slice(h * rb, (h + 1) * rb) for h in range(group)]

    last = hi - 1
    set_bias(last, 1)
    for cols in heads:
        s = scores(last, 1, cols)
        s_s[:, cols] = s
        m_s[0:1, cols] = jnp.max(fold_max(s), axis=0, keepdims=True) * c2
    for cols in heads:
        weigh(last, 1, s_s[:, cols], cols)
    ot_s[...] = dot(vt_s[:, span(last, 1)], u_s[span(last, 1), :])
    blocks(lo, last, attend_step)

    @pl.when(jnp.logical_not(jnp.max(ot_s[HD:HD + 1, :]) < 2.0 ** 60))
    def _():
        m_s[...] = jnp.full_like(m_s, NEG)

        def each_head(step):
            @pl.loop(lo, hi)
            def _(j):
                set_bias(j, 1)

                @pl.loop(0, group)
                def _(h):
                    step(j, pl.ds(pl.multiple_of(h * rb, rb), rb))

        def raise_max(j, cols):
            m_s[:, cols] = jnp.maximum(m_s[:, cols], fold_max(scores(j, 1, cols)))

        def redo(j, cols):
            weigh(j, 1, scores(j, 1, cols), cols)
            ot_s[:, cols] += dot(vt_s[:, span(j, 1)], u_s[span(j, 1), cols])

        each_head(raise_max)
        m_s[0:1, :] = jnp.max(m_s[...], axis=0, keepdims=True) * c2
        ot_s[...] = jnp.zeros_like(ot_s)
        each_head(redo)

    rl = 1.0 / ot_s[HD:HD + 1, :]
    deltas = []
    for h in range(group):
        cols = slice(h * rb, (h + 1) * rb)
        ob = (ot_s[:HD, cols] * rl[:, cols]).astype(BF16)
        o_ref[:, h * HD:(h + 1) * HD] = ob.T
        gt = gt_s[:, cols].astype(F32) * rl[:, cols]
        deltas.append(jnp.sum(ob.astype(F32) * gt, axis=0, keepdims=True))
        gt = gt.astype(BF16)
        gt_s[:, cols] = gt
        gs_s[h * rb:(h + 1) * rb, :] = gt.T

    blocks(lo, hi, grad_step)

    scale = 1.0 / math.sqrt(HD)
    for h in range(group):
        cols = slice(h * rb, (h + 1) * rb)
        dq_ref[:, h * HD:(h + 1) * HD] = (dqt_s[:, cols] * scale).astype(BF16).T

    @pl.when(r == pl.num_programs(0) - 1)
    def _():
        for n, ref in enumerate(dkv_refs):
            at = slice(n * slab, (n + 1) * slab)
            ref[:, :HD] = (dk_s[at, :] * scale).astype(BF16)
            ref[:, HD:] = dv_s[at, :].astype(BF16)


def attend(q, g, kvs, start, lo, chunk, group, prev=None, rb=256):
    rows, width = q.shape
    gw = group * HD
    slab = kvs[0].shape[0]
    nkeys = slab * len(kvs)
    R = group * rb
    n = len(kvs)

    def kernel(*refs):
        if prev is None:
            lo_ref, q_ref, g_ref, *rest = refs
        else:
            lo_ref, q_ref, g_ref, _, _, *rest = refs
        kv_refs, rest = rest[:n], rest[n:]
        start_ref, o_ref, dq_ref, *rest = rest
        body(group, nkeys, lo_ref, q_ref, g_ref, kv_refs, start_ref, o_ref, dq_ref, rest[:n], *rest[n:])

    blk = pl.BlockSpec((rb, gw), lambda r, lo: (r, chunk))
    extra = [] if prev is None else list(prev)
    return pl.pallas_call(
        kernel,
        grid_spec=pltpu.PrefetchScalarGridSpec(
            num_scalar_prefetch=1,
            grid=(rows // rb,),
            in_specs=[blk, blk] + [pl.BlockSpec(memory_space=pl.ANY)] * len(extra)
            + [pl.BlockSpec((slab, 2 * HD), lambda r, lo: (0, 0))] * n
            + [pl.BlockSpec((1, rb), lambda r, lo: (0, r))],
            out_specs=[blk, blk] + [pl.BlockSpec((slab, 2 * HD), lambda r, lo: (0, 0))] * n,
            scratch_shapes=[
                pltpu.VMEM((nkeys, HD), BF16), pltpu.VMEM((nkeys, HD), BF16),
                pltpu.VMEM((HD, nkeys), BF16), pltpu.VMEM((HD + 16, nkeys), BF16),
                pltpu.VMEM((HD, R), BF16), pltpu.VMEM((HD, R), BF16),
                pltpu.VMEM((R, HD), BF16), pltpu.VMEM((R, HD), BF16),
                pltpu.VMEM((KB, R), F32), pltpu.VMEM((nkeys, R), BF16),
                pltpu.VMEM((WIDTHS[0] * KB, rb), F32), pltpu.VMEM((WIDTHS[0] * KB, R), BF16),
                pltpu.VMEM((HD + 16, R), F32), pltpu.VMEM((HD, R), F32),
                pltpu.VMEM((8, R), F32),
                pltpu.VMEM((nkeys, HD), F32), pltpu.VMEM((nkeys, HD), F32),
            ],
        ),
        out_shape=[jax.ShapeDtypeStruct((rows, width), BF16), jax.ShapeDtypeStruct((rows, width), BF16),
                   *[jax.ShapeDtypeStruct((slab, 2 * HD), BF16)] * n],
        input_output_aliases={} if prev is None else {3: 0, 4: 1},
        compiler_params=pltpu.CompilerParams(vmem_limit_bytes=56 * 1024 * 1024),
        name=f"attend{chunk}",
        cost_estimate=pl.CostEstimate(flops=40_000_000_000, bytes_accessed=10_000_000, transcendentals=0),
    )(lo, q, g, *extra, *kvs, start)
def hop(x, shift):
    count = lax.axis_size("ctx")
    return lax.ppermute(x, "ctx", [(s, s + shift) for s in range(count) if 0 <= s + shift < count])


def swap(x):
    return lax.ppermute(x, "ctx", [(s, s ^ 1) for s in range(lax.axis_size("ctx"))])


def after(x, *others):
    return lax.optimization_barrier((x, *others))[0]


def gather_ids(doc_ids):
    tps = lax.axis_size("tp")
    ids = doc_ids[None]
    step = 1
    while step < tps:
        other = lax.ppermute(ids, "tp", [(t, t ^ step) for t in range(tps)])
        low = (lax.axis_index("tp") // step) % 2 == 0
        ids = jnp.where(low, jnp.concatenate([ids, other]), jnp.concatenate([other, ids]))
        step *= 2
    return ids.reshape(-1)


def on_device(queries, keys, values, grad_out, doc_ids):
    slab, width = keys.shape
    chunks = width // HD
    group = queries.shape[1] // width
    me = lax.axis_index("ctx")
    odd = lax.rem(me, 2) == 1
    rb = 256

    def own_part(c):
        return jnp.concatenate([keys[:, c * HD:(c + 1) * HD], values[:, c * HD:(c + 1) * HD]], axis=1)

    own = [own_part(c) for c in range(chunks)]
    two = after(hop(own[0], 2))
    ids = gather_ids(doc_ids)
    earlier = [jnp.where(me >= back, hop(ids, back), -1) for back in (4, 3, 2, 1)]
    four = hop(two, 2)
    one = swap(jnp.where(odd, two, own[0]))
    four, one, earlier, own[1:] = lax.optimization_barrier((four, one, earlier, own[1:]))
    three = swap(jnp.where(odd, four, two))
    ahead = [hop(x, 2) for x in own[1:2]]
    three, ahead, own[1:2] = lax.optimization_barrier((three, ahead, own[1:2]))
    context = jnp.concatenate(earlier + [ids])
    start = jnp.sum((context[:, None] < ids[None, :]).astype(jnp.int32), axis=0)
    lo = start.reshape(slab // rb, rb)[:, 0] // KB
    start = start[None]
    blocks = [four, three, two, one, own[0]]

    outs = None
    grads = []
    for c in range(chunks):
        following = None
        if c + 1 < chunks:
            mine, theirs = own[c + 1], ahead[c] if c < len(ahead) else hop(own[c + 1], 2)
            following = [hop(theirs, 2), hop(theirs, 1), theirs, hop(mine, 1), mine]
        att, gq, *parts = attend(queries, grad_out, blocks, start, lo, c, group, outs, rb)
        outs = (att, gq)
        four_grad, three_grad, two_grad, one_grad, own_grad = parts
        if following is not None:
            back = [hop(four_grad, -4), hop(three_grad, -3), hop(two_grad, -2), hop(one_grad, -1)]
            grads.append([own_grad] + back)
        else:
            f32 = lambda x: x.astype(F32)
            zero = jnp.zeros((slab, 2 * HD), F32)
            swap3 = swap(after(three_grad, *(x for part in grads for x in part)))
            swap1 = f32(swap(after(one_grad, swap3)))
            swap3 = f32(swap3)
            four_grad = (f32(four_grad) + jnp.where(odd, swap3, zero)).astype(BF16)
            two_grad = f32(two_grad) + jnp.where(odd, swap1, swap3)
            two_grad = (two_grad + f32(hop(four_grad, -2))).astype(BF16)
            grads.append([f32(own_grad) + jnp.where(odd, zero, swap1), hop(two_grad, -2)])
        blocks = following
    sums = [sum(x.astype(F32) for x in parts) for parts in grads]
    grad_k = jnp.concatenate([x[:, :HD] for x in sums], axis=1).astype(BF16)
    grad_v = jnp.concatenate([x[:, HD:] for x in sums], axis=1).astype(BF16)
    return outs[0], outs[1], grad_k, grad_v


def solution(mesh):
    return jax.shard_map(
        on_device,
        mesh=mesh,
        in_specs=(P("ctx", "tp"), P("ctx", "tp"), P("ctx", "tp"), P("ctx", "tp"), P(("ctx", "tp"))),
        out_specs=(P("ctx", "tp"), P("ctx", "tp"), P("ctx", "tp"), P("ctx", "tp")),
        check_vma=False,
    )
```

```python
import functools, math
import jax, jax.numpy as jnp
from jax import lax
from jax.sharding import PartitionSpec as P
from jax.experimental import pallas as pl
from jax.experimental.pallas import tpu as pltpu

HD = 128
KB = 256
WIDTHS = (4, 2, 1)
NEG = -1e30
BIG = 1e30
F32, BF16 = jnp.float32, jnp.bfloat16


def dot(a, b):
    return lax.dot_general(a, b, (((1,), (0,)), ((), ())), preferred_element_type=F32)


def body(group, nkeys, slots, lo_ref, q_ref, g_ref, kv_refs, start_ref, o_ref, dq_ref, dkv_refs,
         k_s, v_s, kt_s, vt_s, qt_s, gt_s, qs_s, gs_s, s_s, u_s, bias_s, db_s, ot_s, dqt_s, m_s, dk_s, dv_s):
    r = pl.program_id(0)
    rb = q_ref.shape[0]
    nb = nkeys // KB
    slab = kv_refs[-1].shape[0]
    per = slab // KB
    pairs = [(ref.at[:, :HD], ref.at[:, HD:]) for ref in kv_refs[:-2]] + [tuple(kv_refs[-2:])]
    c2 = math.log2(math.e) / math.sqrt(HD)

    @pl.when(r == 0)
    def _():
        for n, (k_ref, v_ref) in enumerate(pairs):
            for t in range(per):
                at = slice((n * per + t) * KB, (n * per + t + 1) * KB)

                @pl.when(n * per + t >= lo_ref[0])
                def _():
                    k = k_ref[t * KB:(t + 1) * KB, :]
                    v = v_ref[t * KB:(t + 1) * KB, :]
                    k_s[at, :] = k
                    v_s[at, :] = v
                    kt_s[:, at] = k.T
                    vt_s[:HD, at] = v.T
        vt_s[HD:, :] = jnp.ones((vt_s.shape[0] - HD, nkeys), BF16)
        dk_s[...] = jnp.zeros_like(dk_s)
        dv_s[...] = jnp.zeros_like(dv_s)

    for h in range(group):
        q = q_ref[:, h * HD:(h + 1) * HD]
        g = g_ref[:, h * HD:(h + 1) * HD]
        qs_s[h * rb:(h + 1) * rb, :] = q
        qt_s[:, h * rb:(h + 1) * rb] = q.T
        gt_s[:, h * rb:(h + 1) * rb] = g.T

    lo = lo_ref[r]
    hi = nb - pl.num_programs(0) * rb // KB + (r + 1) * rb // KB
    start = start_ref[0:1, :]
    qpos = (nkeys - pl.num_programs(0) * rb) + r * rb + lax.broadcasted_iota(jnp.int32, (1, rb), 1)
    dqt_s[...] = jnp.zeros_like(dqt_s)

    def span(j, wide):
        return pl.ds(pl.multiple_of(j * KB, KB), wide * KB)

    def set_bias(j, wide):
        kpos = j * KB + lax.broadcasted_iota(jnp.int32, (wide * KB, rb), 0)
        bias_s[:wide * KB, :] = jnp.where((kpos >= start) & (kpos <= qpos), BIG, NEG)

    def scores(j, wide, cols):
        return jnp.minimum(dot(k_s[span(j, wide), :], qt_s[:, cols]), bias_s[:wide * KB, :])

    def fold_max(s):
        return jnp.max(s.reshape(KB // 8, 8, rb), axis=0)

    def weigh(j, wide, s, cols):
        u_s[span(j, wide), cols] = jnp.exp2(s * c2 - m_s[0:1, cols]).astype(BF16)

    def attend_step(j, wide):
        set_bias(j, wide)
        for cols in heads:
            weigh(j, wide, scores(j, wide, cols), cols)
        ot_s[...] += dot(vt_s[:, span(j, wide)], u_s[span(j, wide), :])

    def grad_step(j, wide):
        at = span(j, wide)
        for h, cols in enumerate(heads):
            dp = dot(v_s[at, :], gt_s[:, cols])
            db_s[:wide * KB, cols] = (u_s[at, cols].astype(F32) * (dp - deltas[h])).astype(BF16)
        db = db_s[:wide * KB, :]
        dqt_s[...] += dot(kt_s[:, at], db)
        dk_s[at, :] += dot(db, qs_s[...])
        dv_s[at, :] += dot(u_s[at, :], gs_s[...])

    def blocks(first, end, step):
        left = end - first
        for n, wide in enumerate(WIDTHS):
            if n == 0:
                count = left // wide

                @pl.loop(0, count)
                def _(i):
                    step(first + i * wide, wide)

                first, left = first + count * wide, left - count * wide
            else:
                take = left >= wide

                @pl.when(take)
                def _(first=first):
                    step(first, wide)

                first, left = first + jnp.where(take, wide, 0), left - jnp.where(take, wide, 0)

    heads = [slice(h * rb, (h + 1) * rb) for h in range(group)]

    last = hi - 1
    set_bias(last, 1)
    for cols in heads:
        s = scores(last, 1, cols)
        s_s[:, cols] = s
        m_s[0:1, cols] = jnp.max(fold_max(s), axis=0, keepdims=True) * c2
    for cols in heads:
        weigh(last, 1, s_s[:, cols], cols)
    ot_s[...] = dot(vt_s[:, span(last, 1)], u_s[span(last, 1), :])
    blocks(lo, last, attend_step)

    @pl.when(jnp.logical_not(jnp.max(ot_s[HD:HD + 1, :]) < 2.0 ** 60))
    def _():
        m_s[...] = jnp.full_like(m_s, NEG)

        def each_head(step):
            @pl.loop(lo, hi)
            def _(j):
                set_bias(j, 1)

                @pl.loop(0, group)
                def _(h):
                    step(j, pl.ds(pl.multiple_of(h * rb, rb), rb))

        def raise_max(j, cols):
            m_s[:, cols] = jnp.maximum(m_s[:, cols], fold_max(scores(j, 1, cols)))

        def redo(j, cols):
            weigh(j, 1, scores(j, 1, cols), cols)
            ot_s[:, cols] += dot(vt_s[:, span(j, 1)], u_s[span(j, 1), cols])

        each_head(raise_max)
        m_s[0:1, :] = jnp.max(m_s[...], axis=0, keepdims=True) * c2
        ot_s[...] = jnp.zeros_like(ot_s)
        each_head(redo)

    rl = 1.0 / ot_s[HD:HD + 1, :]
    deltas = []
    for h in range(group):
        cols = slice(h * rb, (h + 1) * rb)
        ob = (ot_s[:HD, cols] * rl[:, cols]).astype(BF16)
        o_ref[:, h * HD:(h + 1) * HD] = ob.T
        gt = gt_s[:, cols].astype(F32) * rl[:, cols]
        deltas.append(jnp.sum(ob.astype(F32) * gt, axis=0, keepdims=True))
        gt = gt.astype(BF16)
        gt_s[:, cols] = gt
        gs_s[h * rb:(h + 1) * rb, :] = gt.T

    blocks(lo, hi, grad_step)

    scale = 1.0 / math.sqrt(HD)
    for h in range(group):
        cols = slice(h * rb, (h + 1) * rb)
        dq_ref[:, h * HD:(h + 1) * HD] = (dqt_s[:, cols] * scale).astype(BF16).T

    @pl.when(r == pl.num_programs(0) - 1)
    def _():
        for n, (out, row) in enumerate(slots):
            at = slice(n * slab, (n + 1) * slab)
            rows = slice(row * slab, (row + 1) * slab)
            dkv_refs[out][rows, :HD] = (dk_s[at, :] * scale).astype(BF16)
            dkv_refs[out][rows, HD:] = dv_s[at, :].astype(BF16)


def attend(q, g, kvs, keys, values, start, lo, chunk, group, slots, prev=None, rb=256):
    rows, width = q.shape
    gw = group * HD
    slab = keys.shape[0]
    n = len(kvs) + 1
    nkeys = slab * n
    R = group * rb
    outs = [1 + max(row for out, row in slots if out == o) for o in range(1 + max(out for out, _ in slots))]

    def kernel(*refs):
        if prev is None:
            lo_ref, q_ref, g_ref, *rest = refs
        else:
            lo_ref, q_ref, g_ref, _, _, *rest = refs
        kv_refs, rest = rest[:n + 1], rest[n + 1:]
        start_ref, o_ref, dq_ref, *rest = rest
        body(group, nkeys, slots, lo_ref, q_ref, g_ref, kv_refs, start_ref, o_ref, dq_ref, rest[:len(outs)], *rest[len(outs):])

    blk = pl.BlockSpec((rb, gw), lambda r, lo: (r, chunk))
    extra = [] if prev is None else list(prev)
    return pl.pallas_call(
        kernel,
        grid_spec=pltpu.PrefetchScalarGridSpec(
            num_scalar_prefetch=1,
            grid=(rows // rb,),
            in_specs=[blk, blk] + [pl.BlockSpec(memory_space=pl.ANY)] * len(extra)
            + [pl.BlockSpec((slab, 2 * HD), lambda r, lo: (0, 0))] * (n - 1)
            + [pl.BlockSpec((slab, HD), lambda r, lo: (0, chunk))] * 2
            + [pl.BlockSpec((1, rb), lambda r, lo: (0, r))],
            out_specs=[blk, blk] + [pl.BlockSpec((c * slab, 2 * HD), lambda r, lo: (0, 0)) for c in outs],
            scratch_shapes=[
                pltpu.VMEM((nkeys, HD), BF16), pltpu.VMEM((nkeys, HD), BF16),
                pltpu.VMEM((HD, nkeys), BF16), pltpu.VMEM((HD + 16, nkeys), BF16),
                pltpu.VMEM((HD, R), BF16), pltpu.VMEM((HD, R), BF16),
                pltpu.VMEM((R, HD), BF16), pltpu.VMEM((R, HD), BF16),
                pltpu.VMEM((KB, R), F32), pltpu.VMEM((nkeys, R), BF16),
                pltpu.VMEM((WIDTHS[0] * KB, rb), F32), pltpu.VMEM((WIDTHS[0] * KB, R), BF16),
                pltpu.VMEM((HD + 16, R), F32), pltpu.VMEM((HD, R), F32),
                pltpu.VMEM((8, R), F32),
                pltpu.VMEM((nkeys, HD), F32), pltpu.VMEM((nkeys, HD), F32),
            ],
        ),
        out_shape=[jax.ShapeDtypeStruct((rows, width), BF16), jax.ShapeDtypeStruct((rows, width), BF16),
                   *[jax.ShapeDtypeStruct((c * slab, 2 * HD), BF16) for c in outs]],
        input_output_aliases={} if prev is None else {3: 0, 4: 1},
        compiler_params=pltpu.CompilerParams(vmem_limit_bytes=51 * 1024 * 1024),
        name=f"attend{chunk}",
        cost_estimate=pl.CostEstimate(flops=40_000_000_000, bytes_accessed=10_000_000, transcendentals=0),
    )(lo, q, g, *extra, *kvs, keys, values, start)


def hop(x, shift):
    count = lax.axis_size("ctx")
    return lax.ppermute(x, "ctx", [(s, s + shift) for s in range(count) if 0 <= s + shift < count])


def swap(x):
    return lax.ppermute(x, "ctx", [(s, s ^ 1) for s in range(lax.axis_size("ctx"))])


def after(x, *others):
    return lax.optimization_barrier((x, *others))[0]


def gather_ids(doc_ids):
    tps = lax.axis_size("tp")
    ids = doc_ids[None]
    step = 1
    while step < tps:
        other = lax.ppermute(ids, "tp", [(t, t ^ step) for t in range(tps)])
        low = (lax.axis_index("tp") // step) % 2 == 0
        ids = jnp.where(low, jnp.concatenate([ids, other]), jnp.concatenate([other, ids]))
        step *= 2
    return ids.reshape(-1)


def on_device(queries, keys, values, grad_out, doc_ids):
    slab, width = keys.shape
    chunks = width // HD
    group = queries.shape[1] // width
    me = lax.axis_index("ctx")
    odd = lax.rem(me, 2) == 1
    rb = 256

    def own_part(c):
        return jnp.concatenate([keys[:, c * HD:(c + 1) * HD], values[:, c * HD:(c + 1) * HD]], axis=1)

    own = [own_part(c) for c in range(chunks)]
    two = after(hop(own[0], 2))
    ids = gather_ids(doc_ids)
    earlier = [jnp.where(me >= back, hop(ids, back), -1) for back in (4, 3, 2, 1)]
    four = hop(two, 2)
    one = swap(jnp.where(odd, two, own[0]))
    four, one, own[1:] = lax.optimization_barrier((four, one, own[1:]))
    three = swap(jnp.where(odd, four, two))
    three, earlier = lax.optimization_barrier((three, earlier))
    three, own[1:] = lax.optimization_barrier((three, own[1:]))
    context = jnp.concatenate(earlier + [ids])
    start = jnp.sum((context[:, None] < ids[None, :]).astype(jnp.int32), axis=0)
    lo = start.reshape(slab // rb, rb)[:, 0] // KB
    start = start[None]
    blocks = [four, three, two, one]

    outs = None
    grads = []
    f32 = lambda x: x.astype(F32)
    for c in range(chunks):
        more = c + 1 < chunks
        following = [hop(own[c + 1], back) for back in (4, 3, 2, 1)] if more else None
        slots = tuple((n, 0) for n in range(5))
        att, gq, *parts = attend(queries, grad_out, blocks, keys, values, start, lo, c, group, slots, outs, rb)
        outs = (att, gq)
        four_grad, three_grad, two_grad, one_grad, own_grad = parts
        if more:
            grads.append([own_grad, hop(four_grad, -4), hop(three_grad, -3), hop(two_grad, -2), hop(one_grad, -1)])
        else:
            zero = jnp.zeros((slab, 2 * HD), F32)
            three_grad, grads = lax.optimization_barrier((three_grad, grads))
            swap3 = swap(three_grad)
            swap1 = f32(swap(after(one_grad, swap3)))
            swap3 = f32(swap3)
            four_grad = (f32(four_grad) + jnp.where(odd, swap3, zero)).astype(BF16)
            two_grad = f32(two_grad) + jnp.where(odd, swap1, swap3)
            two_grad = (two_grad + f32(hop(four_grad, -2))).astype(BF16)
            grads.append([f32(own_grad) + jnp.where(odd, zero, swap1), hop(two_grad, -2)])
        blocks = following
    sums = [sum(x.astype(F32) for x in parts) for parts in grads]
    grad_k = jnp.concatenate([x[:, :HD] for x in sums], axis=1).astype(BF16)
    grad_v = jnp.concatenate([x[:, HD:] for x in sums], axis=1).astype(BF16)
    return outs[0], outs[1], grad_k, grad_v


def solution(mesh):
    return jax.shard_map(
        on_device,
        mesh=mesh,
        in_specs=(P("ctx", "tp"), P("ctx", "tp"), P("ctx", "tp"), P("ctx", "tp"), P(("ctx", "tp"))),
        out_specs=(P("ctx", "tp"), P("ctx", "tp"), P("ctx", "tp"), P("ctx", "tp")),
        check_vma=False,
    )
```

```python
import functools, math
import jax, jax.numpy as jnp
from jax import lax
from jax.sharding import PartitionSpec as P
from jax.experimental import pallas as pl
from jax.experimental.pallas import tpu as pltpu

HD = 128
KB = 256
WIDTHS = (4, 2, 1)
NEG = -1e30
BIG = 1e30
F32, BF16 = jnp.float32, jnp.bfloat16


def dot(a, b):
    return lax.dot_general(a, b, (((1,), (0,)), ((), ())), preferred_element_type=F32)


def body(group, nkeys, slots, lo_ref, q_ref, g_ref, kv_refs, start_ref, o_ref, dq_ref, dkv_refs,
         k_s, v_s, kt_s, vt_s, qt_s, gt_s, qs_s, gs_s, s_s, u_s, bias_s, db_s, ot_s, dqt_s, m_s, dk_s, dv_s):
    r = pl.program_id(0)
    rb = q_ref.shape[0]
    nb = nkeys // KB
    slab = kv_refs[-1].shape[0]
    per = slab // KB
    pairs = [(ref.at[:, :HD], ref.at[:, HD:]) for ref in kv_refs[:-2]] + [tuple(kv_refs[-2:])]
    c2 = math.log2(math.e) / math.sqrt(HD)

    @pl.when(r == 0)
    def _():
        for n, (k_ref, v_ref) in enumerate(pairs):
            for t in range(per):
                at = slice((n * per + t) * KB, (n * per + t + 1) * KB)

                @pl.when(n * per + t >= lo_ref[0])
                def _():
                    k = k_ref[t * KB:(t + 1) * KB, :]
                    v = v_ref[t * KB:(t + 1) * KB, :]
                    k_s[at, :] = k
                    v_s[at, :] = v
                    kt_s[:, at] = k.T
                    vt_s[:HD, at] = v.T
        vt_s[HD:, :] = jnp.ones((vt_s.shape[0] - HD, nkeys), BF16)
        dk_s[...] = jnp.zeros_like(dk_s)
        dv_s[...] = jnp.zeros_like(dv_s)

    for h in range(group):
        q = q_ref[:, h * HD:(h + 1) * HD]
        g = g_ref[:, h * HD:(h + 1) * HD]
        qs_s[h * rb:(h + 1) * rb, :] = q
        qt_s[:, h * rb:(h + 1) * rb] = q.T
        gt_s[:, h * rb:(h + 1) * rb] = g.T

    lo = lo_ref[r]
    hi = nb - pl.num_programs(0) * rb // KB + (r + 1) * rb // KB
    start = start_ref[0:1, :]
    qpos = (nkeys - pl.num_programs(0) * rb) + r * rb + lax.broadcasted_iota(jnp.int32, (1, rb), 1)
    dqt_s[...] = jnp.zeros_like(dqt_s)

    def span(j, wide):
        return pl.ds(pl.multiple_of(j * KB, KB), wide * KB)

    def set_bias(j, wide):
        kpos = j * KB + lax.broadcasted_iota(jnp.int32, (wide * KB, rb), 0)
        bias_s[:wide * KB, :] = jnp.where((kpos >= start) & (kpos <= qpos), BIG, NEG)

    def scores(j, wide, cols):
        return jnp.minimum(dot(k_s[span(j, wide), :], qt_s[:, cols]), bias_s[:wide * KB, :])

    def fold_max(s):
        return jnp.max(s.reshape(KB // 8, 8, rb), axis=0)

    def weigh(j, wide, s, cols):
        u_s[span(j, wide), cols] = jnp.exp2(s * c2 - m_s[0:1, cols]).astype(BF16)

    def attend_step(j, wide):
        set_bias(j, wide)
        for cols in heads:
            weigh(j, wide, scores(j, wide, cols), cols)
        ot_s[...] += dot(vt_s[:, span(j, wide)], u_s[span(j, wide), :])

    def grad_step(j, wide):
        at = span(j, wide)
        for h, cols in enumerate(heads):
            dp = dot(v_s[at, :], gt_s[:, cols])
            db_s[:wide * KB, cols] = (u_s[at, cols].astype(F32) * (dp - deltas[h])).astype(BF16)
        db = db_s[:wide * KB, :]
        dqt_s[...] += dot(kt_s[:, at], db)
        dk_s[at, :] += dot(db, qs_s[...])
        dv_s[at, :] += dot(u_s[at, :], gs_s[...])

    def blocks(first, end, step):
        left = end - first
        for n, wide in enumerate(WIDTHS):
            if n == 0:
                count = left // wide

                @pl.loop(0, count)
                def _(i):
                    step(first + i * wide, wide)

                first, left = first + count * wide, left - count * wide
            else:
                take = left >= wide

                @pl.when(take)
                def _(first=first):
                    step(first, wide)

                first, left = first + jnp.where(take, wide, 0), left - jnp.where(take, wide, 0)

    heads = [slice(h * rb, (h + 1) * rb) for h in range(group)]

    last = hi - 1
    set_bias(last, 1)
    for cols in heads:
        s = scores(last, 1, cols)
        s_s[:, cols] = s
        m_s[0:1, cols] = jnp.max(fold_max(s), axis=0, keepdims=True) * c2
    for cols in heads:
        weigh(last, 1, s_s[:, cols], cols)
    ot_s[...] = dot(vt_s[:, span(last, 1)], u_s[span(last, 1), :])
    blocks(lo, last, attend_step)

    @pl.when(jnp.logical_not(jnp.max(ot_s[HD:HD + 1, :]) < 2.0 ** 60))
    def _():
        m_s[...] = jnp.full_like(m_s, NEG)

        def each_head(step):
            @pl.loop(lo, hi)
            def _(j):
                set_bias(j, 1)

                @pl.loop(0, group)
                def _(h):
                    step(j, pl.ds(pl.multiple_of(h * rb, rb), rb))

        def raise_max(j, cols):
            m_s[:, cols] = jnp.maximum(m_s[:, cols], fold_max(scores(j, 1, cols)))

        def redo(j, cols):
            weigh(j, 1, scores(j, 1, cols), cols)
            ot_s[:, cols] += dot(vt_s[:, span(j, 1)], u_s[span(j, 1), cols])

        each_head(raise_max)
        m_s[0:1, :] = jnp.max(m_s[...], axis=0, keepdims=True) * c2
        ot_s[...] = jnp.zeros_like(ot_s)
        each_head(redo)

    rl = 1.0 / ot_s[HD:HD + 1, :]
    deltas = []
    for h in range(group):
        cols = slice(h * rb, (h + 1) * rb)
        ob = (ot_s[:HD, cols] * rl[:, cols]).astype(BF16)
        o_ref[:, h * HD:(h + 1) * HD] = ob.T
        gt = gt_s[:, cols].astype(F32) * rl[:, cols]
        deltas.append(jnp.sum(ob.astype(F32) * gt, axis=0, keepdims=True))
        gt = gt.astype(BF16)
        gt_s[:, cols] = gt
        gs_s[h * rb:(h + 1) * rb, :] = gt.T

    blocks(lo, hi, grad_step)

    scale = 1.0 / math.sqrt(HD)
    for h in range(group):
        cols = slice(h * rb, (h + 1) * rb)
        dq_ref[:, h * HD:(h + 1) * HD] = (dqt_s[:, cols] * scale).astype(BF16).T

    @pl.when(r == pl.num_programs(0) - 1)
    def _():
        for n, (out, row) in enumerate(slots):
            at = slice(n * slab, (n + 1) * slab)
            rows = slice(row * slab, (row + 1) * slab)
            dkv_refs[out][rows, :HD] = (dk_s[at, :] * scale).astype(BF16)
            dkv_refs[out][rows, HD:] = dv_s[at, :].astype(BF16)


def attend(q, g, kvs, keys, values, start, lo, chunk, group, slots, prev=None, rb=256):
    rows, width = q.shape
    gw = group * HD
    slab = keys.shape[0]
    n = len(kvs) + 1
    nkeys = slab * n
    R = group * rb
    outs = [1 + max(row for out, row in slots if out == o) for o in range(1 + max(out for out, _ in slots))]

    def kernel(*refs):
        if prev is None:
            lo_ref, q_ref, g_ref, *rest = refs
        else:
            lo_ref, q_ref, g_ref, _, _, *rest = refs
        kv_refs, rest = rest[:n + 1], rest[n + 1:]
        start_ref, o_ref, dq_ref, *rest = rest
        body(group, nkeys, slots, lo_ref, q_ref, g_ref, kv_refs, start_ref, o_ref, dq_ref, rest[:len(outs)], *rest[len(outs):])

    blk = pl.BlockSpec((rb, gw), lambda r, lo: (r, chunk))
    extra = [] if prev is None else list(prev)
    return pl.pallas_call(
        kernel,
        grid_spec=pltpu.PrefetchScalarGridSpec(
            num_scalar_prefetch=1,
            grid=(rows // rb,),
            in_specs=[blk, blk] + [pl.BlockSpec(memory_space=pl.ANY)] * len(extra)
            + [pl.BlockSpec((slab, 2 * HD), lambda r, lo: (0, 0))] * (n - 1)
            + [pl.BlockSpec((slab, HD), lambda r, lo: (0, chunk))] * 2
            + [pl.BlockSpec((1, rb), lambda r, lo: (0, r))],
            out_specs=[blk, blk] + [pl.BlockSpec((c * slab, 2 * HD), lambda r, lo: (0, 0)) for c in outs],
            scratch_shapes=[
                pltpu.VMEM((nkeys, HD), BF16), pltpu.VMEM((nkeys, HD), BF16),
                pltpu.VMEM((HD, nkeys), BF16), pltpu.VMEM((HD + 16, nkeys), BF16),
                pltpu.VMEM((HD, R), BF16), pltpu.VMEM((HD, R), BF16),
                pltpu.VMEM((R, HD), BF16), pltpu.VMEM((R, HD), BF16),
                pltpu.VMEM((KB, R), F32), pltpu.VMEM((nkeys, R), BF16),
                pltpu.VMEM((WIDTHS[0] * KB, rb), F32), pltpu.VMEM((WIDTHS[0] * KB, R), BF16),
                pltpu.VMEM((HD + 16, R), F32), pltpu.VMEM((HD, R), F32),
                pltpu.VMEM((8, R), F32),
                pltpu.VMEM((nkeys, HD), F32), pltpu.VMEM((nkeys, HD), F32),
            ],
        ),
        out_shape=[jax.ShapeDtypeStruct((rows, width), BF16), jax.ShapeDtypeStruct((rows, width), BF16),
                   *[jax.ShapeDtypeStruct((c * slab, 2 * HD), BF16) for c in outs]],
        input_output_aliases={} if prev is None else {3: 0, 4: 1},
        compiler_params=pltpu.CompilerParams(vmem_limit_bytes=51 * 1024 * 1024),
        name=f"attend{chunk}",
        cost_estimate=pl.CostEstimate(flops=40_000_000_000, bytes_accessed=10_000_000, transcendentals=0),
    )(lo, q, g, *extra, *kvs, keys, values, start)


def hop(x, shift):
    count = lax.axis_size("ctx")
    return lax.ppermute(x, "ctx", [(s, s + shift) for s in range(count) if 0 <= s + shift < count])


def swap(x):
    return lax.ppermute(x, "ctx", [(s, s ^ 1) for s in range(lax.axis_size("ctx"))])


def after(x, *others):
    return lax.optimization_barrier((x, *others))[0]


def gather_ids(doc_ids):
    tps = lax.axis_size("tp")
    ids = doc_ids[None]
    step = 1
    while step < tps:
        other = lax.ppermute(ids, "tp", [(t, t ^ step) for t in range(tps)])
        low = (lax.axis_index("tp") // step) % 2 == 0
        ids = jnp.where(low, jnp.concatenate([ids, other]), jnp.concatenate([other, ids]))
        step *= 2
    return ids.reshape(-1)


def on_device(queries, keys, values, grad_out, doc_ids):
    slab, width = keys.shape
    chunks = width // HD
    group = queries.shape[1] // width
    me = lax.axis_index("ctx")
    odd = lax.rem(me, 2) == 1
    rb = 256

    def own_part(c):
        return jnp.concatenate([keys[:, c * HD:(c + 1) * HD], values[:, c * HD:(c + 1) * HD]], axis=1)

    own = [own_part(c) for c in range(chunks)]
    two = after(hop(own[0], 2))
    ids = gather_ids(doc_ids)
    near = [jnp.where(me >= back, hop(ids, back), -1) for back in (2, 1)]
    far = jnp.where(me >= 2, hop(jnp.concatenate(near), 2), -1)
    earlier = [far] + near
    four = hop(two, 2)
    one = swap(jnp.where(odd, two, own[0]))
    four, one, own[1:] = lax.optimization_barrier((four, one, own[1:]))
    three = swap(jnp.where(odd, four, two))
    three, earlier = lax.optimization_barrier((three, earlier))
    three, own[1:] = lax.optimization_barrier((three, own[1:]))
    context = jnp.concatenate(earlier + [ids])
    start = jnp.sum((context[:, None] < ids[None, :]).astype(jnp.int32), axis=0)
    lo = start.reshape(slab // rb, rb)[:, 0] // KB
    start = start[None]
    blocks = [four, three, two, one]

    outs = None
    grads = []
    f32 = lambda x: x.astype(F32)
    for c in range(chunks):
        more = c + 1 < chunks
        following = [hop(own[c + 1], back) for back in (4, 3, 2, 1)] if more else None
        slots = tuple((n, 0) for n in range(5))
        att, gq, *parts = attend(queries, grad_out, blocks, keys, values, start, lo, c, group, slots, outs, rb)
        outs = (att, gq)
        four_grad, three_grad, two_grad, one_grad, own_grad = parts
        if more:
            grads.append([own_grad, hop(four_grad, -4), hop(three_grad, -3), hop(two_grad, -2), hop(one_grad, -1)])
        else:
            zero = jnp.zeros((slab, 2 * HD), F32)
            three_grad, grads = lax.optimization_barrier((three_grad, grads))
            swap3 = swap(three_grad)
            swap1 = f32(swap(after(one_grad, swap3)))
            swap3 = f32(swap3)
            four_grad = (f32(four_grad) + jnp.where(odd, swap3, zero)).astype(BF16)
            two_grad = f32(two_grad) + jnp.where(odd, swap1, swap3)
            two_grad = (two_grad + f32(hop(four_grad, -2))).astype(BF16)
            grads.append([f32(own_grad) + jnp.where(odd, zero, swap1), hop(two_grad, -2)])
        blocks = following
    sums = [sum(x.astype(F32) for x in parts) for parts in grads]
    grad_k = jnp.concatenate([x[:, :HD] for x in sums], axis=1).astype(BF16)
    grad_v = jnp.concatenate([x[:, HD:] for x in sums], axis=1).astype(BF16)
    return outs[0], outs[1], grad_k, grad_v


def solution(mesh):
    return jax.shard_map(
        on_device,
        mesh=mesh,
        in_specs=(P("ctx", "tp"), P("ctx", "tp"), P("ctx", "tp"), P("ctx", "tp"), P(("ctx", "tp"))),
        out_specs=(P("ctx", "tp"), P("ctx", "tp"), P("ctx", "tp"), P("ctx", "tp")),
        check_vma=False,
    )
```

```python
import functools, math
import jax, jax.numpy as jnp
from jax import lax
from jax.sharding import PartitionSpec as P
from jax.experimental import pallas as pl
from jax.experimental.pallas import tpu as pltpu

HD = 128
KB = 256
WIDTHS = (4, 2, 1)
NEG = -1e30
BIG = 1e30
F32, BF16 = jnp.float32, jnp.bfloat16


def dot(a, b):
    return lax.dot_general(a, b, (((1,), (0,)), ((), ())), preferred_element_type=F32)


def body(group, nkeys, slots, lo_ref, q_ref, g_ref, kv_refs, start_ref, o_ref, dq_ref, dkv_refs,
         k_s, v_s, kt_s, vt_s, qt_s, gt_s, qs_s, gs_s, s_s, u_s, bias_s, db_s, ot_s, dqt_s, m_s, dk_s, dv_s):
    r = pl.program_id(0)
    rb = q_ref.shape[0]
    nb = nkeys // KB
    slab = kv_refs[-1].shape[0]
    per = slab // KB
    pairs = [(ref.at[:, :HD], ref.at[:, HD:]) for ref in kv_refs[:-2]] + [tuple(kv_refs[-2:])]
    c2 = math.log2(math.e) / math.sqrt(HD)

    @pl.when(r == 0)
    def _():
        for n, (k_ref, v_ref) in enumerate(pairs):
            for t in range(per):
                at = slice((n * per + t) * KB, (n * per + t + 1) * KB)

                @pl.when(n * per + t >= lo_ref[0])
                def _():
                    k = k_ref[t * KB:(t + 1) * KB, :]
                    v = v_ref[t * KB:(t + 1) * KB, :]
                    k_s[at, :] = k
                    v_s[at, :] = v
                    kt_s[:, at] = k.T
                    vt_s[:HD, at] = v.T
        vt_s[HD:, :] = jnp.ones((vt_s.shape[0] - HD, nkeys), BF16)
        dk_s[...] = jnp.zeros_like(dk_s)
        dv_s[...] = jnp.zeros_like(dv_s)

    for h in range(group):
        q = q_ref[:, h * HD:(h + 1) * HD]
        g = g_ref[:, h * HD:(h + 1) * HD]
        qs_s[h * rb:(h + 1) * rb, :] = q
        qt_s[:, h * rb:(h + 1) * rb] = q.T
        gt_s[:, h * rb:(h + 1) * rb] = g.T

    lo = lo_ref[r]
    hi = nb - pl.num_programs(0) * rb // KB + (r + 1) * rb // KB
    start = start_ref[0:1, :]
    qpos = (nkeys - pl.num_programs(0) * rb) + r * rb + lax.broadcasted_iota(jnp.int32, (1, rb), 1)
    dqt_s[...] = jnp.zeros_like(dqt_s)

    def span(j, wide):
        return pl.ds(pl.multiple_of(j * KB, KB), wide * KB)

    def set_bias(j, wide):
        kpos = j * KB + lax.broadcasted_iota(jnp.int32, (wide * KB, rb), 0)
        bias_s[:wide * KB, :] = jnp.where((kpos >= start) & (kpos <= qpos), BIG, NEG)

    def scores(j, wide, cols):
        return jnp.minimum(dot(k_s[span(j, wide), :], qt_s[:, cols]), bias_s[:wide * KB, :])

    def fold_max(s):
        return jnp.max(s.reshape(KB // 8, 8, rb), axis=0)

    def weigh(j, wide, s, cols):
        u_s[span(j, wide), cols] = jnp.exp2(s * c2 - m_s[0:1, cols]).astype(BF16)

    def attend_step(j, wide):
        set_bias(j, wide)
        for cols in heads:
            weigh(j, wide, scores(j, wide, cols), cols)
        ot_s[...] += dot(vt_s[:, span(j, wide)], u_s[span(j, wide), :])

    def grad_step(j, wide):
        at = span(j, wide)
        for h, cols in enumerate(heads):
            dp = dot(v_s[at, :], gt_s[:, cols])
            db_s[:wide * KB, cols] = (u_s[at, cols].astype(F32) * (dp - deltas[h])).astype(BF16)
        db = db_s[:wide * KB, :]
        dqt_s[...] += dot(kt_s[:, at], db)
        dk_s[at, :] += dot(db, qs_s[...])
        dv_s[at, :] += dot(u_s[at, :], gs_s[...])

    def blocks(first, end, step):
        left = end - first
        for n, wide in enumerate(WIDTHS):
            if n == 0:
                count = left // wide

                @pl.loop(0, count)
                def _(i):
                    step(first + i * wide, wide)

                first, left = first + count * wide, left - count * wide
            else:
                take = left >= wide

                @pl.when(take)
                def _(first=first):
                    step(first, wide)

                first, left = first + jnp.where(take, wide, 0), left - jnp.where(take, wide, 0)

    heads = [slice(h * rb, (h + 1) * rb) for h in range(group)]

    last = hi - 1
    set_bias(last, 1)
    for cols in heads:
        s = scores(last, 1, cols)
        s_s[:, cols] = s
        m_s[0:1, cols] = jnp.max(fold_max(s), axis=0, keepdims=True) * c2
    for cols in heads:
        weigh(last, 1, s_s[:, cols], cols)
    ot_s[...] = dot(vt_s[:, span(last, 1)], u_s[span(last, 1), :])
    blocks(lo, last, attend_step)

    @pl.when(jnp.logical_not(jnp.max(ot_s[HD:HD + 1, :]) < 2.0 ** 60))
    def _():
        m_s[...] = jnp.full_like(m_s, NEG)

        def each_head(step):
            @pl.loop(lo, hi)
            def _(j):
                set_bias(j, 1)

                @pl.loop(0, group)
                def _(h):
                    step(j, pl.ds(pl.multiple_of(h * rb, rb), rb))

        def raise_max(j, cols):
            m_s[:, cols] = jnp.maximum(m_s[:, cols], fold_max(scores(j, 1, cols)))

        def redo(j, cols):
            weigh(j, 1, scores(j, 1, cols), cols)
            ot_s[:, cols] += dot(vt_s[:, span(j, 1)], u_s[span(j, 1), cols])

        each_head(raise_max)
        m_s[0:1, :] = jnp.max(m_s[...], axis=0, keepdims=True) * c2
        ot_s[...] = jnp.zeros_like(ot_s)
        each_head(redo)

    rl = 1.0 / ot_s[HD:HD + 1, :]
    deltas = []
    for h in range(group):
        cols = slice(h * rb, (h + 1) * rb)
        ob = (ot_s[:HD, cols] * rl[:, cols]).astype(BF16)
        o_ref[:, h * HD:(h + 1) * HD] = ob.T
        gt = gt_s[:, cols].astype(F32) * rl[:, cols]
        deltas.append(jnp.sum(ob.astype(F32) * gt, axis=0, keepdims=True))
        gt = gt.astype(BF16)
        gt_s[:, cols] = gt
        gs_s[h * rb:(h + 1) * rb, :] = gt.T

    blocks(lo, hi, grad_step)

    scale = 1.0 / math.sqrt(HD)
    for h in range(group):
        cols = slice(h * rb, (h + 1) * rb)
        dq_ref[:, h * HD:(h + 1) * HD] = (dqt_s[:, cols] * scale).astype(BF16).T

    @pl.when(r == pl.num_programs(0) - 1)
    def _():
        for n, (out, row) in enumerate(slots):
            at = slice(n * slab, (n + 1) * slab)
            rows = slice(row * slab, (row + 1) * slab)
            dkv_refs[out][rows, :HD] = (dk_s[at, :] * scale).astype(BF16)
            dkv_refs[out][rows, HD:] = dv_s[at, :].astype(BF16)


def attend(q, g, kvs, keys, values, start, lo, chunk, group, slots, prev=None, rb=256):
    rows, width = q.shape
    gw = group * HD
    slab = keys.shape[0]
    n = len(kvs) + 1
    nkeys = slab * n
    R = group * rb
    outs = [1 + max(row for out, row in slots if out == o) for o in range(1 + max(out for out, _ in slots))]

    def kernel(*refs):
        if prev is None:
            lo_ref, q_ref, g_ref, *rest = refs
        else:
            lo_ref, q_ref, g_ref, _, _, *rest = refs
        kv_refs, rest = rest[:n + 1], rest[n + 1:]
        start_ref, o_ref, dq_ref, *rest = rest
        body(group, nkeys, slots, lo_ref, q_ref, g_ref, kv_refs, start_ref, o_ref, dq_ref, rest[:len(outs)], *rest[len(outs):])

    blk = pl.BlockSpec((rb, gw), lambda r, lo: (r, chunk))
    extra = [] if prev is None else list(prev)
    return pl.pallas_call(
        kernel,
        grid_spec=pltpu.PrefetchScalarGridSpec(
            num_scalar_prefetch=1,
            grid=(rows // rb,),
            in_specs=[blk, blk] + [pl.BlockSpec(memory_space=pl.ANY)] * len(extra)
            + [pl.BlockSpec((slab, 2 * HD), lambda r, lo: (0, 0))] * (n - 1)
            + [pl.BlockSpec((slab, HD), lambda r, lo: (0, chunk))] * 2
            + [pl.BlockSpec((1, rb), lambda r, lo: (0, r))],
            out_specs=[blk, blk] + [pl.BlockSpec((c * slab, 2 * HD), lambda r, lo: (0, 0)) for c in outs],
            scratch_shapes=[
                pltpu.VMEM((nkeys, HD), BF16), pltpu.VMEM((nkeys, HD), BF16),
                pltpu.VMEM((HD, nkeys), BF16), pltpu.VMEM((HD + 16, nkeys), BF16),
                pltpu.VMEM((HD, R), BF16), pltpu.VMEM((HD, R), BF16),
                pltpu.VMEM((R, HD), BF16), pltpu.VMEM((R, HD), BF16),
                pltpu.VMEM((KB, R), F32), pltpu.VMEM((nkeys, R), BF16),
                pltpu.VMEM((WIDTHS[0] * KB, rb), F32), pltpu.VMEM((WIDTHS[0] * KB, R), BF16),
                pltpu.VMEM((HD + 16, R), F32), pltpu.VMEM((HD, R), F32),
                pltpu.VMEM((8, R), F32),
                pltpu.VMEM((nkeys, HD), F32), pltpu.VMEM((nkeys, HD), F32),
            ],
        ),
        out_shape=[jax.ShapeDtypeStruct((rows, width), BF16), jax.ShapeDtypeStruct((rows, width), BF16),
                   *[jax.ShapeDtypeStruct((c * slab, 2 * HD), BF16) for c in outs]],
        input_output_aliases={} if prev is None else {3: 0, 4: 1},
        compiler_params=pltpu.CompilerParams(vmem_limit_bytes=51 * 1024 * 1024),
        name=f"attend{chunk}",
        cost_estimate=pl.CostEstimate(flops=40_000_000_000, bytes_accessed=10_000_000, transcendentals=0),
    )(lo, q, g, *extra, *kvs, keys, values, start)


def hop(x, shift):
    count = lax.axis_size("ctx")
    return lax.ppermute(x, "ctx", [(s, s + shift) for s in range(count) if 0 <= s + shift < count])


def swap(x):
    return lax.ppermute(x, "ctx", [(s, s ^ 1) for s in range(lax.axis_size("ctx"))])


def after(x, *others):
    return lax.optimization_barrier((x, *others))[0]


def gather_ids(doc_ids):
    tps = lax.axis_size("tp")
    ids = doc_ids[None]
    step = 1
    while step < tps:
        other = lax.ppermute(ids, "tp", [(t, t ^ step) for t in range(tps)])
        low = (lax.axis_index("tp") // step) % 2 == 0
        ids = jnp.where(low, jnp.concatenate([ids, other]), jnp.concatenate([other, ids]))
        step *= 2
    return ids.reshape(-1)


def on_device(queries, keys, values, grad_out, doc_ids):
    slab, width = keys.shape
    chunks = width // HD
    group = queries.shape[1] // width
    me = lax.axis_index("ctx")
    odd = lax.rem(me, 2) == 1
    rb = 256

    def own_part(c):
        return jnp.concatenate([keys[:, c * HD:(c + 1) * HD], values[:, c * HD:(c + 1) * HD]], axis=1)

    own = [own_part(c) for c in range(chunks)]
    two = after(hop(own[0], 2))
    ids = gather_ids(doc_ids)
    near = [jnp.where(me >= back, hop(ids, back), -1) for back in (2, 1)]
    far = jnp.where(me >= 2, hop(jnp.concatenate(near), 2), -1)
    earlier = [far] + near
    four = hop(two, 2)
    one = swap(jnp.where(odd, two, own[0]))
    four, one, own[1:] = lax.optimization_barrier((four, one, own[1:]))
    three = swap(jnp.where(odd, four, two))
    three, earlier = lax.optimization_barrier((three, earlier))
    three, own[1:] = lax.optimization_barrier((three, own[1:]))
    context = jnp.concatenate(earlier + [ids])
    start = jnp.sum((context[:, None] < ids[None, :]).astype(jnp.int32), axis=0)
    lo = start.reshape(slab // rb, rb)[:, 0] // KB
    start = start[None]
    blocks = [four, three, two, one]

    outs = None
    sent = []
    grads = []
    f32 = lambda x: x.astype(F32)
    for c in range(chunks):
        more = c + 1 < chunks
        following = [hop(own[c + 1], back) for back in (4, 3, 2, 1)] if more else None
        slots = ((0, 0), (1, 0), (0, 1), (1, 1), (2, 0)) if more else ((0, 0), (1, 0), (2, 0), (3, 0), (4, 0))
        att, gq, *parts = attend(queries, grad_out, blocks, keys, values, start, lo, c, group, slots, outs, rb)
        outs = (att, gq)
        if more:
            even_pair, odd_pair, own_grad = parts
            even_pair, odd_pair = hop(even_pair, -2), hop(odd_pair, -1)
            sent.append((even_pair, odd_pair))
            grads.append([own_grad, even_pair[slab:], odd_pair[slab:]])
        else:
            four_grad, three_grad, two_grad, one_grad, own_grad = parts
            zero = jnp.zeros((slab, 2 * HD), F32)
            three_grad, sent = lax.optimization_barrier((three_grad, sent))
            swap3 = swap(three_grad)
            on = [hop((f32(even[:slab]) + f32(odd_[:slab])).astype(BF16), -2) for even, odd_ in sent]
            grads = [part + [x] for part, x in zip(grads, on)]
            swap1 = f32(swap(after(one_grad, swap3)))
            swap3 = f32(swap3)
            four_grad = (f32(four_grad) + jnp.where(odd, swap3, zero)).astype(BF16)
            two_grad = f32(two_grad) + jnp.where(odd, swap1, swap3)
            two_grad = after(two_grad + f32(hop(four_grad, -2)), *on).astype(BF16)
            grads.append([f32(own_grad) + jnp.where(odd, zero, swap1), hop(two_grad, -2)])
        blocks = following
    sums = [sum(x.astype(F32) for x in parts) for parts in grads]
    grad_k = jnp.concatenate([x[:, :HD] for x in sums], axis=1).astype(BF16)
    grad_v = jnp.concatenate([x[:, HD:] for x in sums], axis=1).astype(BF16)
    return outs[0], outs[1], grad_k, grad_v


def solution(mesh):
    return jax.shard_map(
        on_device,
        mesh=mesh,
        in_specs=(P("ctx", "tp"), P("ctx", "tp"), P("ctx", "tp"), P("ctx", "tp"), P(("ctx", "tp"))),
        out_specs=(P("ctx", "tp"), P("ctx", "tp"), P("ctx", "tp"), P("ctx", "tp")),
        check_vma=False,
    )
```
